256 devices in a mesh: row: 16 (over y, z_lo, core), col: 16 (over z_hi, x).
Axes of the slice: x: 4, y: 4, z: 8 (z_hi: 4, z_lo: 2; z = z_hi * 2 + z_lo), core: 2. Of those that a mesh axis runs over, the one named last changes fastest.
Arguments:
- field: bfloat16 [2, 1024, 1024, 256], P(None, 'row', 'col'), may hold values from -6 to 6
- phases: float32 [4, 1024, 1024], P(None, 'row', 'col'), may hold values from -3.140625 to 3.140625
- frequencies: float32 [4, 256], replicated, may hold values from 0.5 to 2
- self_mats: bfloat16 [4, 2, 2, 64, 64], replicated, may hold values from -0.375 to 0.375
- cross_mats: bfloat16 [4, 2, 2, 64, 64], replicated, may hold values from -0.375 to 0.375
- plane_mats: bfloat16 [4, 2, 64, 64], replicated, may hold values from -0.5 to 0.5
Outputs:
- result: bfloat16 [2, 1024, 1024, 256], P(None, 'row', 'col')
The draws below stay inside these ranges and needn't reach their ends.
All inputs are finite; a program needn't handle non-finite values.
Results may differ from the reference program's by a relative error of at most 0.018.
Values may be sent and summed in bfloat16 or wider, within the bound.
A program may use at most 128 MiB of HBM per device.

```python
import math
import jax
import jax.numpy as jnp
import numpy as np
from jax import lax

RANK = 64
BLOCKS = 4
LEVELS = 4
PLANES = 256
NR = 1024
NC = 1024
N_ROW = 16
N_COL = 16


def block_scale(own_key, extent, pieces, least, high):
    gain, own = 1.0, jax.random.fold_in(own_key, 6)
    for position, shards_of in pieces:
        steps = jnp.exp(jax.random.uniform(jax.random.fold_in(own, position), (shards_of,), jnp.float32, least / len(pieces), high / len(pieces)))
        gain = gain * jnp.repeat(steps, extent[position] // shards_of).reshape([-1 if axis == position else 1 for axis in range(len(extent))])
    return gain


def bell_draw(own_key, dims, scale, bound, split=(), kind=jnp.bfloat16):
    array = jax.random.normal(own_key, dims, jnp.float32) * scale
    if len(split) > 0:
        array = block_scale(own_key, dims, split, -0.22, 0.18) * array
    return jnp.clip(array, min=-bound, max=bound).astype(kind)


def setup_inputs(seed: int = 0) -> dict:
    key_of = jax.random.split(jax.random.key(seed), 7)
    field = bell_draw(key_of[0], (2, NR, NC, PLANES), 1.0, 6.0, ((1, 16), (2, 16)))
    phases = jnp.clip(jax.random.uniform(key_of[1], (LEVELS, NR, NC), jnp.float32, -3.140625, 3.140625), -3.140625, 3.140625)
    frequencies = jnp.clip(jnp.exp(jax.random.uniform(key_of[2], (LEVELS, PLANES), jnp.float32, math.log(0.5), math.log(2.0))), 0.5, 2.0)
    self_mats = bell_draw(key_of[3], (LEVELS, 2, 2, RANK, RANK), (4 * RANK) ** -0.5, 0.375)
    cross_mats = bell_draw(key_of[4], (LEVELS, 2, 2, RANK, RANK), (4 * RANK) ** -0.5, 0.375)
    plane_mats = bell_draw(key_of[5], (LEVELS, 2, RANK, RANK), (2 * RANK) ** -0.5, 0.5)
    return {"field": field, "phases": phases, "frequencies": frequencies, "self_mats": self_mats, "cross_mats": cross_mats, "plane_mats": plane_mats}


def complex_apply(matrices, values):
    def single(matrix, operand):
        return jnp.einsum('nab,nbcq->nacq', matrix, operand)
    real_part = single(matrices[:, 0], values[0]) - single(matrices[:, 1], values[1])
    imag_part = single(matrices[:, 0], values[1]) + single(matrices[:, 1], values[0])
    return real_part, imag_part


def level_first(volume, angles, freq, self_level, cross_level, plane_level, bit_index):
    groups = volume.shape[1] // RANK
    devices = np.arange(groups)
    partner = devices ^ (1 << bit_index)
    halves = (devices >> bit_index) & 1
    values = volume.astype(jnp.float32).reshape(2, groups, RANK, volume.shape[2], volume.shape[3])
    partner_values = values[:, partner]
    self_pick = self_level.astype(jnp.float32)[halves]
    cross_pick = cross_level.astype(jnp.float32)[halves]
    self_real, self_imag = complex_apply(self_pick, values)
    cross_real, cross_imag = complex_apply(cross_pick, partner_values)
    shape = (volume.shape[1], volume.shape[2], volume.shape[3])
    sum_real = (self_real + cross_real).reshape(shape)
    sum_imag = (self_imag + cross_imag).reshape(shape)
    theta = angles[:, :, None] * freq[None, None, :]
    cosine = jnp.cos(theta)
    sine = jnp.sin(theta)
    turned = jnp.stack([cosine * sum_real - sine * sum_imag, sine * sum_real + cosine * sum_imag]).astype(jnp.bfloat16)
    plane_f = plane_level.astype(jnp.float32)
    turned_f = turned.astype(jnp.float32)
    out_real = jnp.einsum('sq,rcq->rcs', plane_f[0], turned_f[0]) - jnp.einsum('sq,rcq->rcs', plane_f[1], turned_f[1])
    out_imag = jnp.einsum('sq,rcq->rcs', plane_f[0], turned_f[1]) + jnp.einsum('sq,rcq->rcs', plane_f[1], turned_f[0])
    return jnp.stack([out_real, out_imag]).astype(jnp.bfloat16)


def one_block(volume, freqs, phases, self_mats, cross_mats, plane_mats):
    row_top = N_ROW.bit_length() - 2
    col_top = N_COL.bit_length() - 2
    plan = [(0, row_top), (1, col_top), (0, 0), (1, 0)]
    for level in range(LEVELS):
        which, bit_index = plan[level]
        if which == 0:
            volume = level_first(volume, phases[level], freqs[level], self_mats[level], cross_mats[level], plane_mats[level], bit_index)
        else:
            swapped = level_first(jnp.swapaxes(volume, 1, 2), phases[level].T, freqs[level], self_mats[level], cross_mats[level], plane_mats[level], bit_index)
            volume = jnp.swapaxes(swapped, 1, 2)
    return volume


def reference(field, phases, frequencies, self_mats, cross_mats, plane_mats):
    blocked = field.reshape(2, NR, NC, BLOCKS, RANK).transpose(3, 0, 1, 2, 4)
    freq_blocked = frequencies.reshape(LEVELS, BLOCKS, RANK).transpose(1, 0, 2)
    done = lax.map(lambda pair: one_block(pair[0], pair[1], phases, self_mats, cross_mats, plane_mats), (blocked, freq_blocked))
    return done.transpose(1, 2, 3, 0, 4).reshape(2, NR, NC, PLANES)
```

```python
import functools

import jax
import jax.numpy as jnp
from jax import lax
from jax.experimental import pallas as pl
from jax.experimental.pallas import tpu as pltpu
from jax.sharding import PartitionSpec as P

MESH = pl.DeviceIdType.MESH
F32 = jnp.float32
BF16 = jnp.bfloat16
R = 64
N = 8
Q = R // N
W = 3
SINE = (
    6.283182621002197,
    -41.34142303466797,
    81.59618377685547,
    -76.5801010131836,
    41.20539093017578,
    -12.27125358581543,
)


def kernel(
    x, phases, freqs, selfs, crosses, planes, out,
    stage, a, s, y, f, g, b2s, b2r, b3s, b3r, zb, tab, ostage, zphase, mats, mixes,
    in_sem, ph_s, ph_r, zf_s, zf_r, y_s, y_r, c_s, c_r, x_s, x_r, zb_s, zb_r, out_sem,
):
    gr, gc = lax.axis_index("row"), lax.axis_index("col")
    nr, nc = lax.axis_size("row"), lax.axis_size("col")
    half = (gr // (nr // 2), gc // (nc // 2), gr % 2, gc % 2)
    to_y = (gr + nr // 2 - nr * half[0], gc)
    to_z = (gr, gc + nc // 2 - nc * half[1])
    to_c = (gr + 1 - 2 * half[2], gc)
    to_x = (gr, gc + 1 - 2 * half[3])

    def lanes_of(which):
        return pl.ds(pl.multiple_of(which * 2 * R, 2 * R), 2 * R)

    mine, theirs = lanes_of(half[1]), lanes_of(1 - half[1])

    def load_copy(n, side, lanes):
        return pltpu.make_async_copy(
            x.at[:, :, pl.ds(pl.multiple_of(n * 16, 16), 16), lanes],
            stage.at[side * 4 + n], in_sem.at[side * 4 + n])

    def remote(src, dst, ssem, rsem, to):
        return pltpu.make_async_remote_copy(
            src_ref=src, dst_ref=dst, send_sem=ssem, recv_sem=rsem,
            device_id=to, device_id_type=MESH)

    def phase_copy():
        return remote(phases, zphase, ph_s, ph_r, to_z)

    def z_fwd(i):
        return remote(s.at[i], a.at[1, i], zf_s.at[i], zf_r.at[i], to_z)

    def y_copy(grp, i):
        n = grp * 2 * N + i
        return remote(a.at[grp, i], y.at[grp, i], y_s.at[n], y_r.at[n], to_y)

    def c_copy(grp, u, j):
        n = grp * 2 * N + u * N + j
        return remote(b2s.at[grp, j], b2r.at[grp, u * N + j], c_s.at[n], c_r.at[n], to_c)

    def x_copy(grp, u, j):
        n = grp * 2 * N + u * N + j
        return remote(b3s.at[grp, j], b3r.at[grp, u * N + j], x_s.at[n], x_r.at[n], to_x)

    def z_back(i):
        return remote(s.at[i], zb.at[i], zb_s.at[i], zb_r.at[i], to_z)

    def out_copy(side, j, lanes):
        return pltpu.make_async_copy(
            ostage.at[side * N + j],
            out.at[:, pl.ds(pl.multiple_of(j * Q, Q), Q), :, lanes],
            out_sem.at[side * N + j])

    def loop(n, body):
        lax.fori_loop(0, n, lambda i, c: (body(i), c)[1], 0)

    for n in range(4):
        load_copy(n, 0, theirs).start()
    for n in range(4):
        load_copy(n, 1, mine).start()

    barrier = pltpu.get_barrier_semaphore()
    for to in (to_y, to_z, to_c, to_x):
        pl.semaphore_signal(barrier, inc=1, device_id=to, device_id_type=MESH)
    pl.semaphore_wait(barrier, 4)
    phase_copy().start()

    lane = lax.broadcasted_iota(jnp.int32, (R, 2 * R), 1)
    low = lane < R

    def turn(v):
        return pltpu.roll(v, R, 1)

    def pack(n, side, put):
        f[0, pl.ds(0, R * 16)] = stage[side * 4 + n, 0].reshape(R * 16, 2 * R).astype(F32)
        f[1, pl.ds(0, R * 16)] = stage[side * 4 + n, 1].reshape(R * 16, 2 * R).astype(F32)
        for k in range(16):
            re = f[0, pl.ds(k, R, stride=16)]
            im = f[1, pl.ds(k, R, stride=16)]
            put(n * 2 + k // Q, k % Q,
                jnp.where(low, re, turn(im)).astype(BF16),
                jnp.where(low, turn(re), im).astype(BF16))

    def put_s(j, k, first, second):
        s[j, k] = first
        s[N + j, k] = second

    def put_a(j, k, first, second):
        a[0, j, k] = first
        a[0, N + j, k] = second

    def pack_theirs(n):
        load_copy(n, 0, theirs).wait()
        pack(n, 0, put_s)

    def pack_mine(n):
        load_copy(n, 1, mine).wait()
        pack(n, 1, put_a)
        y_copy(0, 2 * n).start()
        y_copy(0, 2 * n + 1).start()

    pack_theirs(0)
    z_fwd(0).start()
    z_fwd(1).start()
    pack_theirs(1)
    z_fwd(2).start()
    loop(2, lambda n: pack_theirs(n + 2))
    loop(4, pack_mine)

    for k in range(4):
        h = half[k]
        own = selfs[k, h]
        far = crosses[k, h]
        if k == 1:
            own2 = selfs[k, 1 - h]
            far2 = crosses[k, 1 - h]
            rows = [(own, far), (far2, own2)]
        else:
            rows = [(own, far)]
        blocks = []
        for left, right in rows:
            for part in range(2):
                blocks.append(jnp.concatenate(
                    [left[part].astype(F32), right[part].astype(F32)], axis=1))
        m = jnp.concatenate(blocks, axis=0)
        mats[k, pl.ds(0, m.shape[0])] = m.astype(BF16)
        re, im = planes[k, 0].astype(F32), planes[k, 1].astype(F32)
        wide = jnp.concatenate([
            jnp.concatenate([re, -im, -im, -re], axis=1),
            jnp.concatenate([im, re, re, -im], axis=1)], axis=0)
        mixes[k] = wide.T.astype(BF16)

    sub = lax.broadcasted_iota(jnp.int32, (R, R), 0)
    col = lax.broadcasted_iota(jnp.int32, (R, R), 1)
    quarter = jnp.where(low, 0.0, 0.25)

    def table(k, grp, j):
        ph = phases if grp == 0 else zphase
        fr = freqs[pl.ds(k, 1), mine] * (0.5 / jnp.pi)
        low1 = lax.broadcasted_iota(jnp.int32, (1, 2 * R), 1) < R
        frs = (jnp.where(low1, fr, turn(fr)), jnp.where(low1, turn(fr), fr))

        def one(q):
            o = j * Q + q
            if k % 2 == 0:
                picked = jnp.where(col == o, ph[k], 0.0)
            else:
                picked = jnp.where(col == sub, ph[k, pl.ds(o, 1)], 0.0)
            angle = jnp.sum(picked, axis=1, keepdims=True)
            for u in range(2):
                t = angle * frs[u] + quarter
                t = t - jnp.round(t)
                t2 = t * t
                p = SINE[5]
                for c in SINE[4::-1]:
                    p = p * t2 + c
                tab[k, grp, u * N + j, q] = (p * t).astype(BF16)

        for q in range(Q):
            one(q)

    def rotate(k, grp, i, q, p_, q_):
        t = tab[k, grp, i, q].astype(F32)
        r = turn(t)
        sine = jnp.where(low, t, r)
        cosine = jnp.where(low, r, t)
        return jnp.concatenate(
            [(cosine * p_ - sine * q_).astype(BF16), (sine * p_ + cosine * q_).astype(BF16)],
            axis=1)

    def mix(k, rows):
        return jnp.dot(jnp.concatenate(rows, axis=0), mixes[k], preferred_element_type=F32)

    def apart(k, grp, i, own, far, put):
        m = mats[k, pl.ds(0, 2 * R)]
        for q in range(0, Q, 2):
            v = [jnp.concatenate([own[q + d], far[q + d]], axis=0) for d in range(2)]
            pq = jnp.dot(m, jnp.concatenate(v, axis=1), preferred_element_type=F32)
            rows = [
                rotate(k, grp, i, q + d, pq[:R, d * 2 * R:(d + 1) * 2 * R],
                       pq[R:, d * 2 * R:(d + 1) * 2 * R])
                for d in range(2)]
            v = mix(k, rows)
            for d in range(2):
                put(q + d, v[d * R:(d + 1) * R])

    def row_of(o):
        return pl.ds(pl.multiple_of(o * R, R), R)

    def put_f(grp, j):
        def put(q, v):
            f[grp, row_of(j * Q + q)] = v
        return put

    def level0(grp, u, j):
        i = u * N + j
        y_copy(grp, i).wait()
        apart(0, grp, i, a.at[grp, i], y.at[grp, i], put_f(grp, j))

    def level1(u, j):
        m = mats[1]
        for q in range(0, Q, 2):
            v = []
            for d in range(2):
                o = j * Q + q + d
                v.append(jnp.concatenate(
                    [f[grp, pl.ds(o, R, stride=R)].astype(BF16) for grp in range(2)], axis=0))
            pq = jnp.dot(m, jnp.concatenate(v, axis=1), preferred_element_type=F32)
            for grp in range(2):
                rows = [
                    rotate(1, grp, u * N + j, q + d,
                           pq[grp * 2 * R:grp * 2 * R + R, d * 2 * R:(d + 1) * 2 * R],
                           pq[grp * 2 * R + R:(grp + 1) * 2 * R, d * 2 * R:(d + 1) * 2 * R])
                    for d in range(2)]
                w = mix(1, rows)
                for d in range(2):
                    g[grp, row_of(j * Q + q + d)] = w[d * R:(d + 1) * R]

    def core_send(u, j):
        for grp in range(2):
            for q in range(Q):
                b2s[grp, j, q] = g[grp, pl.ds(j * Q + q, R, stride=R)].astype(BF16)
            c_copy(grp, u, j).start()

    def level2(u, j):
        for grp in range(2):
            c_copy(grp, u, j).wait()
            apart(2, grp, u * N + j, b2s.at[grp, j], b2r.at[grp, u * N + j], put_f(grp, j))

    def x_pack(grp, j):
        for q in range(Q):
            b3s[grp, j, q] = f[grp, pl.ds(j * Q + q, R, stride=R)].astype(BF16)

    def x_send(u, j):
        x_pack(1, j)
        x_copy(1, u, j).start()
        x_pack(0, j)

    def level3(grp, u, j):
        i = u * N + j
        dst = a.at[0, i] if grp == 0 else s.at[i]

        def put(q, v):
            dst[q] = v.astype(BF16)

        x_copy(grp, u, j).wait()
        apart(3, grp, i, b3s.at[grp, j], b3r.at[grp, i], put)

    def merge(first, second, side, j, lanes):
        for q in range(Q):
            p0, p1 = first[q].astype(F32), second[q].astype(F32)
            ostage[side * N + j, 0, q] = jnp.where(low, p0, turn(p1)).astype(BF16)
            ostage[side * N + j, 1, q] = jnp.where(low, turn(p0), p1).astype(BF16)
        out_copy(side, j, lanes).start()

    def z_arrive(i, more):
        z_fwd(i).wait()
        if more:
            z_fwd(i + W).start()
        y_copy(1, i).start()

    phase_copy().wait()

    def come0(j):
        for k in range(4):
            table(k, 0, j)
            table(k, 1, j)
        level0(0, 0, j)
        z_arrive(j, True)

    come0(0)

    def come(j):
        come0(j + 1)
        level0(1, 0, j)

    loop(N - 1, come)
    loop(N, lambda j: y_copy(0, N + j).start())
    level0(1, 0, N - 1)

    loop(N // 2, lambda j: level1(0, j))
    z_arrive(N, True)
    loop(N // 2, lambda j: level1(0, j + N // 2))
    z_arrive(N + 1, True)
    loop(N, lambda j: core_send(0, j))
    loop(N, lambda j: level2(0, j))
    z_arrive(N + 2, True)
    loop(N, lambda j: x_send(0, j))
    z_arrive(N + 3, True)
    loop(N, lambda j: level0(0, 1, j))

    def come1(j):
        z_arrive(N + 4 + j, False)
        level0(1, 1, j)
        for d in range(2):
            level3(1, 0, 2 * j + d)
            x_copy(0, 0, 2 * j + d).start()

    z_arrive(N + 4, True)
    level0(1, 1, 0)
    level3(1, 0, 0)
    x_copy(0, 0, 0).start()
    level3(1, 0, 1)
    x_copy(0, 0, 1).start()
    loop(1, lambda _: come1(1))
    z_back(0).start()
    loop(1, lambda _: come1(2))
    z_back(1).start()
    loop(1, lambda _: come1(3))
    loop(N - 2, lambda j: z_back(j + 2).start())
    loop(N - 4, lambda j: level0(1, 1, j + 4))

    loop(N, lambda j: level1(1, j))
    loop(N, lambda j: core_send(1, j))
    loop(N, lambda j: level2(1, j))
    loop(N, lambda j: level3(0, 0, j))
    loop(N, lambda j: x_send(1, j))

    def back1(j):
        level3(1, 1, j)
        z_back(N + j).start()
        x_copy(0, 1, j).start()

    loop(N, back1)

    def own1(j):
        level3(0, 1, j)
        merge(a.at[0, j], a.at[0, N + j], 0, j, mine)

    loop(N, own1)

    def last(j):
        z_back(j).wait()
        z_back(N + j).wait()
        merge(zb.at[j], zb.at[N + j], 1, j, theirs)

    loop(N, last)
    loop(N, lambda j: out_copy(0, j, mine).wait())
    loop(N, lambda j: out_copy(1, j, theirs).wait())


def local(field, phases, frequencies, self_mats, cross_mats, plane_mats):
    vm = pl.BlockSpec(memory_space=pltpu.VMEM)
    anywhere = pl.BlockSpec(memory_space=pl.ANY)
    chunk = (Q, R, 2 * R)
    unit2 = (2 * N,) + chunk
    dma = pltpu.SemaphoreType.DMA
    return pl.pallas_call(
        kernel,
        out_shape=jax.ShapeDtypeStruct(field.shape, field.dtype),
        in_specs=[anywhere, vm, vm, vm, vm, vm],
        out_specs=anywhere,
        scratch_shapes=[
            pltpu.VMEM((8, 2, R, 16, 2 * R), BF16),
            pltpu.VMEM((2,) + unit2, BF16),
            pltpu.VMEM(unit2, BF16),
            pltpu.VMEM((2,) + unit2, BF16),
            pltpu.VMEM((2, R * R, 2 * R), F32),
            pltpu.VMEM((2, R * R, 2 * R), F32),
            pltpu.VMEM((2, N) + chunk, BF16),
            pltpu.VMEM((2,) + unit2, BF16),
            pltpu.VMEM((2, N) + chunk, BF16),
            pltpu.VMEM((2,) + unit2, BF16),
            pltpu.VMEM(unit2, BF16),
            pltpu.VMEM((4, 2) + unit2, BF16),
            pltpu.VMEM((2 * N, 2) + chunk, BF16),
            pltpu.VMEM((4, R, R), F32),
            pltpu.VMEM((4, 4 * R, 2 * R), BF16),
            pltpu.VMEM((4, 4 * R, 2 * R), BF16),
            dma((8,)), dma, dma, dma((2 * N,)), dma((2 * N,)),
            dma((4 * N,)), dma((4 * N,)), dma((4 * N,)), dma((4 * N,)),
            dma((4 * N,)), dma((4 * N,)), dma((2 * N,)), dma((2 * N,)), dma((2 * N,)),
        ],
        compiler_params=pltpu.CompilerParams(
            collective_id=0, has_side_effects=True, vmem_limit_bytes=62 * 2**20),
        cost_estimate=pl.CostEstimate(
            flops=12 * 2**30, bytes_accessed=2**23, transcendentals=2**23),
    )(field, phases, frequencies, self_mats, cross_mats, plane_mats)


def solution(mesh):
    return jax.shard_map(
        local,
        mesh=mesh,
        in_specs=(P(None, "row", "col", None), P(None, "row", "col"), P(), P(), P(), P()),
        out_specs=P(None, "row", "col", None),
        check_vma=False,
    )
```

```python
import functools

import jax
import jax.numpy as jnp
from jax import lax
from jax.experimental import pallas as pl
from jax.experimental.pallas import tpu as pltpu
from jax.sharding import PartitionSpec as P

MESH = pl.DeviceIdType.MESH
F32 = jnp.float32
BF16 = jnp.bfloat16
R = 64
N = 8
Q = R // N
SINE = (
    6.283182621002197,
    -41.34142303466797,
    81.59618377685547,
    -76.5801010131836,
    41.20539093017578,
    -12.27125358581543,
)


def kernel(
    x, phases_in, freqs, selfs_in, crosses_in, planes_in, out,
    phases, selfs, crosses, planes, ownphase, stage, a, s, y, f, g, b2s, b2r, b3s, b3r, zb, tab, zphase, mats, mixes,
    in_sem, ph_s, ph_r, zf_s, zf_r, y_s, y_r, c_s, c_r, x_s, x_r, zb_s, zb_r, mat_sem, gate,
):
    gr, gc = lax.axis_index("row"), lax.axis_index("col")
    nr, nc = lax.axis_size("row"), lax.axis_size("col")
    half = (gr // (nr // 2), gc // (nc // 2), gr % 2, gc % 2)
    to_y = (gr + nr // 2 - nr * half[0], gc)
    to_z = (gr, gc + nc // 2 - nc * half[1])
    to_c = (gr + 1 - 2 * half[2], gc)
    to_x = (gr, gc + 1 - 2 * half[3])
    other = (gr, (gc + nc // 4) % nc)
    late = (gc // (nc // 4)) % 2
    other_back = (gr, (gc + nc - nc // 4) % nc)

    def lanes_of(which):
        return pl.ds(pl.multiple_of(which * 2 * R, 2 * R), 2 * R)

    mine, theirs = lanes_of(half[1]), lanes_of(1 - half[1])

    def load_copy(n, side, lanes):
        return pltpu.make_async_copy(
            x.at[:, :, pl.ds(pl.multiple_of(n * 16, 16), 16), lanes],
            stage.at[side * 4 + n], in_sem.at[side * 4 + n])

    def remote(src, dst, ssem, rsem, to):
        return pltpu.make_async_remote_copy(
            src_ref=src, dst_ref=dst, send_sem=ssem, recv_sem=rsem,
            device_id=to, device_id_type=MESH)

    def phase_copy():
        return remote(ownphase, zphase, ph_s, ph_r, to_z)

    def small_copy(n):
        src = (phases_in, selfs_in, crosses_in, planes_in)[n]
        dst = (phases, selfs, crosses, planes)[n]
        return pltpu.make_async_copy(src, dst, mat_sem.at[n])

    def z_fwd(i):
        return remote(s.at[i], a.at[1, i], zf_s.at[i], zf_r.at[i], to_z)

    def y_copy(grp, i):
        n = grp * 2 * N + i
        return remote(a.at[grp, i], y.at[grp, i], y_s.at[n], y_r.at[n], to_y)

    def c_copy(grp, u, j):
        n = grp * 2 * N + u * N + j
        return remote(b2s.at[grp, j], b2r.at[grp, u * N + j], c_s.at[n], c_r.at[n], to_c)

    def x_copy(grp, u, j):
        n = grp * 2 * N + u * N + j
        return remote(b3s.at[grp, j], b3r.at[grp, u * N + j], x_s.at[n], x_r.at[n], to_x)

    def z_back(i):
        return remote(s.at[i], zb.at[i], zb_s.at[i], zb_r.at[i], to_z)

    def loop(n, body):
        lax.fori_loop(0, n, lambda i, c: (body(i), c)[1], 0)

    load_copy(0, 0, theirs).start()
    small_copy(0).start()
    for n in range(1, 4):
        load_copy(n, 0, theirs).start()
    for n in range(4):
        load_copy(n, 1, mine).start()
    for n in range(1, 4):
        small_copy(n).start()

    barrier = pltpu.get_barrier_semaphore()
    for to in (to_y, to_z, to_c, to_x, other, other_back):
        pl.semaphore_signal(barrier, inc=1, device_id=to, device_id_type=MESH)

    lane = lax.broadcasted_iota(jnp.int32, (R, 2 * R), 1)
    low = lane < R

    def turn(v):
        return pltpu.roll(v, R, 1)

    def pack(n, side, put):
        f[0, pl.ds(0, R * 16)] = stage[side * 4 + n, 0].reshape(R * 16, 2 * R).astype(F32)
        f[1, pl.ds(0, R * 16)] = stage[side * 4 + n, 1].reshape(R * 16, 2 * R).astype(F32)
        for k in range(16):
            re = f[0, pl.ds(k, R, stride=16)]
            im = f[1, pl.ds(k, R, stride=16)]
            put(n * 2 + k // Q, k % Q,
                jnp.where(low, re, turn(im)).astype(BF16),
                jnp.where(low, turn(re), im).astype(BF16))

    def put_s(j, k, first, second):
        s[j, k] = first
        s[N + j, k] = second

    def put_a(j, k, first, second):
        a[0, j, k] = first
        a[0, N + j, k] = second

    def pack_theirs(n):
        load_copy(n, 0, theirs).wait()
        pack(n, 0, put_s)

    def pack_mine(n):
        load_copy(n, 1, mine).wait()
        pack(n, 1, put_a)
        y_copy(0, 2 * n).start()
        y_copy(0, 2 * n + 1).start()

    pack_theirs(0)
    pl.semaphore_wait(barrier, 6)

    @pl.when(late == 0)
    def _():
        z_fwd(0).start()
        z_fwd(1).start()

    small_copy(0).wait()
    for k in range(2):
        ownphase[k] = jnp.concatenate([phases[2 * k], phases[2 * k + 1]], axis=1)
    phase_copy().start()

    def pack_next(n):
        pack_theirs(n + 1)

        @pl.when(late == 0)
        def _():
            z_fwd(2 * n + 2).start()
            z_fwd(2 * n + 3).start()

    loop(3, pack_next)

    @pl.when(late == 0)
    def _():
        loop(N, lambda j: z_fwd(N + j).start())

    loop(4, pack_mine)

    for n in range(1, 4):
        small_copy(n).wait()
    for k in range(4):
        h = half[k]
        own = selfs[k, h]
        far = crosses[k, h]
        if k == 1:
            own2 = selfs[k, 1 - h]
            far2 = crosses[k, 1 - h]
            rows = [(own, far), (far2, own2)]
        else:
            rows = [(own, far)]
        blocks = []
        for left, right in rows:
            for part in range(2):
                blocks.append(jnp.concatenate(
                    [left[part].astype(F32), right[part].astype(F32)], axis=1))
        m = jnp.concatenate(blocks, axis=0)
        mats[k, pl.ds(0, m.shape[0])] = m.astype(BF16)
        re, im = planes[k, 0].astype(F32), planes[k, 1].astype(F32)
        wide = jnp.concatenate([
            jnp.concatenate([re, -im, -im, -re], axis=1),
            jnp.concatenate([im, re, re, -im], axis=1)], axis=0)
        mixes[k] = wide.T.astype(BF16)

    sub = lax.broadcasted_iota(jnp.int32, (R, 2 * R), 0)
    quarter = jnp.where(low, 0.0, 0.25)

    def table(k, grp, j):
        ph = ownphase if grp == 0 else zphase
        first = k % 2 * R
        fr = freqs[pl.ds(k, 1), mine] * (0.5 / jnp.pi)
        low1 = lax.broadcasted_iota(jnp.int32, (1, 2 * R), 1) < R
        frs = (jnp.where(low1, fr, turn(fr)), jnp.where(low1, turn(fr), fr))

        def one(q):
            o = j * Q + q
            if k % 2 == 0:
                picked = jnp.where(lane == o + first, ph[k // 2], 0.0)
            else:
                picked = jnp.where(lane == sub + first, ph[k // 2, pl.ds(o, 1)], 0.0)
            angle = jnp.sum(picked, axis=1, keepdims=True)
            for u in range(2):
                t = angle * frs[u] + quarter
                t = t - jnp.round(t)
                t2 = t * t
                p = SINE[5]
                for c in SINE[4::-1]:
                    p = p * t2 + c
                tab[k, grp, u * N + j, q] = (p * t).astype(BF16)

        def some(n):
            for d in range(4):
                one(4 * n + d)

        loop(Q // 4, some)

    def rotate(k, grp, i, q, p_, q_):
        t = tab[k, grp, i, q].astype(F32)
        r = turn(t)
        sine = jnp.where(low, t, r)
        cosine = jnp.where(low, r, t)
        return jnp.concatenate(
            [(cosine * p_ - sine * q_).astype(BF16), (sine * p_ + cosine * q_).astype(BF16)],
            axis=1)

    def mix(k, rows):
        return jnp.dot(jnp.concatenate(rows, axis=0), mixes[k], preferred_element_type=F32)

    def apart(k, grp, i, own, far, put):
        m = mats[k, pl.ds(0, 2 * R)]

        def pair(q):
            v = [jnp.concatenate([own[q + d], far[q + d]], axis=0) for d in range(2)]
            pq = jnp.dot(m, jnp.concatenate(v, axis=1), preferred_element_type=F32)
            rows = [
                rotate(k, grp, i, q + d, pq[:R, d * 2 * R:(d + 1) * 2 * R],
                       pq[R:, d * 2 * R:(d + 1) * 2 * R])
                for d in range(2)]
            v = mix(k, rows)
            for d in range(2):
                put(q + d, v[d * R:(d + 1) * R])

        for q in range(0, Q, 2):
            pair(q)

    def row_of(o):
        return pl.ds(pl.multiple_of(o * R, R), R)

    def put_f(grp, j):
        def put(q, v):
            f[grp, row_of(j * Q + q)] = v
        return put

    def level0(grp, u, j):
        i = u * N + j
        y_copy(grp, i).wait()
        apart(0, grp, i, a.at[grp, i], y.at[grp, i], put_f(grp, j))

    def level1(u, j):
        m = mats[1]

        def pair(n):
            q = 2 * n
            v = []
            for d in range(2):
                o = j * Q + q + d
                v.append(jnp.concatenate(
                    [f[grp, pl.ds(o, R, stride=R)].astype(BF16) for grp in range(2)], axis=0))
            pq = jnp.dot(m, jnp.concatenate(v, axis=1), preferred_element_type=F32)
            for grp in range(2):
                rows = [
                    rotate(1, grp, u * N + j, q + d,
                           pq[grp * 2 * R:grp * 2 * R + R, d * 2 * R:(d + 1) * 2 * R],
                           pq[grp * 2 * R + R:(grp + 1) * 2 * R, d * 2 * R:(d + 1) * 2 * R])
                    for d in range(2)]
                w = mix(1, rows)
                for d in range(2):
                    g[grp, row_of(j * Q + q + d)] = w[d * R:(d + 1) * R]

        for n in range(Q // 2):
            pair(n)

    def core_send(u, j):
        for grp in range(2):
            for q in range(Q):
                b2s[grp, j, q] = g[grp, pl.ds(j * Q + q, R, stride=R)].astype(BF16)
            c_copy(grp, u, j).start()

    def level2(u, j):
        for grp in range(2):
            c_copy(grp, u, j).wait()
            apart(2, grp, u * N + j, b2s.at[grp, j], b2r.at[grp, u * N + j], put_f(grp, j))

    def x_pack(grp, j):
        for q in range(Q):
            b3s[grp, j, q] = f[grp, pl.ds(j * Q + q, R, stride=R)].astype(BF16)

    def x_send(u, j):
        x_pack(1, j)
        x_copy(1, u, j).start()
        x_pack(0, j)

    def level3(grp, u, j):
        i = u * N + j
        dst = a.at[0, i] if grp == 0 else s.at[i]

        def put(q, v):
            dst[q] = v.astype(BF16)

        x_copy(grp, u, j).wait()
        apart(3, grp, i, b3s.at[grp, j], b3r.at[grp, i], put)

    def merge(first, second, side, j, lanes):
        for q in range(Q):
            p0, p1 = first[q].astype(F32), second[q].astype(F32)
            out[0, j * Q + q, :, lanes] = jnp.where(low, p0, turn(p1)).astype(BF16)
            out[1, j * Q + q, :, lanes] = jnp.where(low, turn(p0), p1).astype(BF16)

    def z_arrive(i):
        z_fwd(i).wait()
        y_copy(1, i).start()

    def early(j):
        for k in range(4):
            table(k, 0, j)
        level0(0, 0, j)

    loop(N, early)

    @pl.when(late == 1)
    def _():
        pl.semaphore_wait(gate, 1)
        loop(2 * N, lambda i: z_fwd(i).start())

    phase_copy().wait()

    def come(j):
        z_arrive(j)

        @pl.when((late == 0) & (j == 0))
        def _():
            pl.semaphore_signal(gate, inc=1, device_id=other, device_id_type=MESH)

        for k in range(4):
            table(k, 1, j)

        @pl.when(j > 0)
        def _():
            level0(1, 0, j - 1)

    loop(N, come)
    loop(N, lambda j: y_copy(0, N + j).start())
    level0(1, 0, N - 1)

    loop(N, lambda j: level1(0, j))
    loop(4, lambda j: z_arrive(N + j))
    loop(N, lambda j: core_send(0, j))
    loop(N, lambda j: level2(0, j))
    loop(3, lambda j: z_arrive(N + 4 + j))
    loop(N, lambda j: x_send(0, j))
    z_arrive(2 * N - 1)
    loop(N, lambda j: level0(0, 1, j))

    def back0(j):
        level3(1, 0, j)
        z_back(j).start()
        x_copy(0, 0, j).start()

    loop(N, back0)
    loop(N, lambda j: level0(1, 1, j))

    loop(N, lambda j: level1(1, j))
    loop(N, lambda j: core_send(1, j))
    loop(N, lambda j: level2(1, j))
    loop(N, lambda j: level3(0, 0, j))
    loop(N, lambda j: x_send(1, j))

    def back1(j):
        level3(1, 1, j)
        z_back(N + j).start()
        x_copy(0, 1, j).start()

    loop(N, back1)

    def own1(j):
        level3(0, 1, j)
        merge(a.at[0, j], a.at[0, N + j], 0, j, mine)

    loop(N, own1)

    def last(j):
        z_back(j).wait()
        z_back(N + j).wait()
        merge(zb.at[j], zb.at[N + j], 1, j, theirs)

    loop(N, last)


def flush(src, dst, sem):
    copies = []
    for n in range(2 * N):
        part = (n // N, pl.ds(n % N * Q, Q))
        copies.append(pltpu.make_async_copy(src.at[part], dst.at[part], sem.at[n]))
    for copy in copies:
        copy.start()
    for copy in copies:
        copy.wait()


def local(field, phases, frequencies, self_mats, cross_mats, plane_mats):
    vm = pl.BlockSpec(memory_space=pltpu.VMEM)
    anywhere = pl.BlockSpec(memory_space=pl.ANY)
    chunk = (Q, R, 2 * R)
    unit2 = (2 * N,) + chunk
    dma = pltpu.SemaphoreType.DMA
    result = pl.pallas_call(
        kernel,
        out_shape=pltpu.VMEM(field.shape, field.dtype),
        in_specs=[anywhere, anywhere, vm, anywhere, anywhere, anywhere],
        out_specs=vm,
        scratch_shapes=[
            pltpu.VMEM(phases.shape, F32),
            pltpu.VMEM(self_mats.shape, BF16),
            pltpu.VMEM(cross_mats.shape, BF16),
            pltpu.VMEM(plane_mats.shape, BF16),
            pltpu.VMEM((2, R, 2 * R), F32),
            pltpu.VMEM((8, 2, R, 16, 2 * R), BF16),
            pltpu.VMEM((2,) + unit2, BF16),
            pltpu.VMEM(unit2, BF16),
            pltpu.VMEM((2,) + unit2, BF16),
            pltpu.VMEM((2, R * R, 2 * R), F32),
            pltpu.VMEM((2, R * R, 2 * R), F32),
            pltpu.VMEM((2, N) + chunk, BF16),
            pltpu.VMEM((2,) + unit2, BF16),
            pltpu.VMEM((2, N) + chunk, BF16),
            pltpu.VMEM((2,) + unit2, BF16),
            pltpu.VMEM(unit2, BF16),
            pltpu.VMEM((4, 2) + unit2, BF16),
            pltpu.VMEM((2, R, 2 * R), F32),
            pltpu.VMEM((4, 4 * R, 2 * R), BF16),
            pltpu.VMEM((4, 4 * R, 2 * R), BF16),
            dma((8,)), dma, dma, dma((2 * N,)), dma((2 * N,)),
            dma((4 * N,)), dma((4 * N,)), dma((4 * N,)), dma((4 * N,)),
            dma((4 * N,)), dma((4 * N,)), dma((2 * N,)), dma((2 * N,)),
            dma((4,)), pltpu.SemaphoreType.REGULAR,
        ],
        compiler_params=pltpu.CompilerParams(
            collective_id=0, has_side_effects=True, vmem_limit_bytes=58 * 2**20),
        cost_estimate=pl.CostEstimate(
            flops=12 * 2**30, bytes_accessed=2**23, transcendentals=2**23),
    )(field, phases, frequencies, self_mats, cross_mats, plane_mats)
    return pl.pallas_call(
        flush,
        out_shape=jax.ShapeDtypeStruct(field.shape, field.dtype),
        in_specs=[vm],
        out_specs=anywhere,
        scratch_shapes=[dma((2 * N,))],
        cost_estimate=pl.CostEstimate(flops=0, bytes_accessed=2**22, transcendentals=0),
    )(result)


def solution(mesh):
    return jax.shard_map(
        local,
        mesh=mesh,
        in_specs=(P(None, "row", "col", None), P(None, "row", "col"), P(), P(), P(), P()),
        out_specs=P(None, "row", "col", None),
        check_vma=False,
    )
```

```python
import functools

import jax
import jax.numpy as jnp
from jax import lax
from jax.experimental import pallas as pl
from jax.experimental.pallas import tpu as pltpu
from jax.sharding import PartitionSpec as P

MESH = pl.DeviceIdType.MESH
F32 = jnp.float32
BF16 = jnp.bfloat16
R = 64
N = 8
Q = R // N
SINE = (
    6.283182621002197,
    -41.34142303466797,
    81.59618377685547,
    -76.5801010131836,
    41.20539093017578,
    -12.27125358581543,
)


def kernel(
    x, phases_in, freqs_in, selfs_in, crosses_in, planes_in, out,
    phases, freqs, selfs, crosses, planes, ownphase, a, s, y, f, g, b2r, b3r, zb, tab, zphase, mats, mixes,
    in_sem, ph_s, ph_r, zf_s, zf_r, y_s, y_r, c_s, c_r, x_s, x_r, zb_s, zb_r, mat_sem, gate,
):
    gr, gc = lax.axis_index("row"), lax.axis_index("col")
    nr, nc = lax.axis_size("row"), lax.axis_size("col")
    half = (gr // (nr // 2), gc // (nc // 2), gr % 2, gc % 2)
    to_y = (gr + nr // 2 - nr * half[0], gc)
    to_z = (gr, gc + nc // 2 - nc * half[1])
    to_c = (gr + 1 - 2 * half[2], gc)
    to_x = (gr, gc + 1 - 2 * half[3])
    other = (gr, (gc + nc // 4) % nc)
    late = (gc // (nc // 4)) % 2
    other_back = (gr, (gc + nc - nc // 4) % nc)

    def lanes_of(which):
        return pl.ds(pl.multiple_of(which * 2 * R, 2 * R), 2 * R)

    mine, theirs = lanes_of(half[1]), lanes_of(1 - half[1])

    def load_copy(n, side, lanes):
        return pltpu.make_async_copy(
            x.at[:, :, pl.ds(pl.multiple_of(n * 16, 16), 16), lanes],
            tab.at[side * 4 + n], in_sem.at[side * 4 + n])

    def remote(src, dst, ssem, rsem, to):
        return pltpu.make_async_remote_copy(
            src_ref=src, dst_ref=dst, send_sem=ssem, recv_sem=rsem,
            device_id=to, device_id_type=MESH)

    def phase_copy():
        return remote(ownphase, zphase, ph_s, ph_r, to_z)

    def small_copy(n):
        src = (phases_in, freqs_in, selfs_in, crosses_in, planes_in)[n]
        dst = (phases, freqs, selfs, crosses, planes)[n]
        return pltpu.make_async_copy(src, dst, mat_sem.at[n])

    def z_fwd(i):
        return remote(s.at[i], a.at[1, i], zf_s.at[i], zf_r.at[i], to_z)

    def y_copy(grp, i):
        return remote(a.at[grp, i], y.at[grp, i], y_s.at[i], y_r.at[i], to_y)

    def y_own(n):
        part = (0, pl.ds(2 * n, 2))
        return remote(a.at[part], y.at[part], y_s.at[2 * N + n], y_r.at[2 * N + n], to_y)

    def c_copy(u, j):
        n = u * N + j
        return remote(y.at[:, n], b2r.at[:, n], c_s.at[n], c_r.at[n], to_c)

    def x_copy(grp, u, j):
        n = grp * 2 * N + u * N + j
        return remote(a.at[grp, u * N + j], b3r.at[grp, u * N + j], x_s.at[n], x_r.at[n], to_x)

    def z_back(i):
        return remote(s.at[i], zb.at[i], zb_s.at[i], zb_r.at[i], to_z)

    def loop(n, body):
        lax.fori_loop(0, n, lambda i, c: (body(i), c)[1], 0)

    small_copy(0).start()
    for n in range(4):
        load_copy(n, 0, theirs).start()
    for n in range(4):
        load_copy(n, 1, mine).start()
    for n in range(1, 5):
        small_copy(n).start()

    barrier = pltpu.get_barrier_semaphore()
    for to in (to_y, to_z, to_c, to_x, other, other_back):
        pl.semaphore_signal(barrier, inc=1, device_id=to, device_id_type=MESH)

    lane = lax.broadcasted_iota(jnp.int32, (R, 2 * R), 1)
    low = lane < R

    def turn(v):
        return pltpu.roll(v, R, 1)

    def pack(n, side, put):
        f[0, pl.ds(0, R * 16)] = tab[side * 4 + n, 0].reshape(R * 16, 2 * R).astype(F32)
        f[1, pl.ds(0, R * 16)] = tab[side * 4 + n, 1].reshape(R * 16, 2 * R).astype(F32)
        for k in range(16):
            re = f[0, pl.ds(k, R, stride=16)]
            im = f[1, pl.ds(k, R, stride=16)]
            put(n * 2 + k // Q, k % Q,
                jnp.where(low, re, turn(im)).astype(BF16),
                jnp.where(low, turn(re), im).astype(BF16))

    def put_s(j, k, first, second):
        s[j, k] = first
        s[N + j, k] = second

    def put_a(j, k, first, second):
        a[0, j, k] = first
        a[0, N + j, k] = second

    def pack_theirs(n):
        load_copy(n, 0, theirs).wait()
        pack(n, 0, put_s)

    def pack_mine(n):
        load_copy(n, 1, mine).wait()
        pack(n, 1, put_a)
        y_own(n).start()

    small_copy(0).wait()
    for k in range(2):
        ownphase[k] = jnp.concatenate([phases[2 * k], phases[2 * k + 1]], axis=1)
    pl.semaphore_wait(barrier, 6)
    phase_copy().start()
    pack_theirs(0)

    @pl.when(late == 0)
    def _():
        z_fwd(0).start()
        z_fwd(1).start()

    def pack_next(n):
        pack_theirs(n + 1)

        @pl.when(late == 0)
        def _():
            z_fwd(2 * n + 2).start()
            z_fwd(2 * n + 3).start()

    loop(3, pack_next)

    @pl.when(late == 0)
    def _():
        loop(N, lambda j: z_fwd(N + j).start())

    loop(4, pack_mine)

    for n in range(1, 5):
        small_copy(n).wait()
    for k in range(4):
        h = half[k]
        own = selfs[k, h]
        far = crosses[k, h]
        if k == 1:
            own2 = selfs[k, 1 - h]
            far2 = crosses[k, 1 - h]
            rows = [(own, far), (far2, own2)]
        else:
            rows = [(own, far)]
        blocks = []
        for left, right in rows:
            for part in range(2):
                blocks.append(jnp.concatenate(
                    [left[part].astype(F32), right[part].astype(F32)], axis=1))
        m = jnp.concatenate(blocks, axis=0)
        mats[k, pl.ds(0, m.shape[0])] = m.astype(BF16)
        re, im = planes[k, 0].astype(F32), planes[k, 1].astype(F32)
        wide = jnp.concatenate([
            jnp.concatenate([re, -im, -im, -re], axis=1),
            jnp.concatenate([im, re, re, -im], axis=1)], axis=0)
        mixes[k] = wide.T.astype(BF16)

    sub = lax.broadcasted_iota(jnp.int32, (R, 2 * R), 0)
    quarter = jnp.where(low, 0.0, 0.25)

    def tab_at(k, grp, j, q):
        return ((k * 2 + grp) * 2 + j // 4, j // 2 % 2, pl.ds(j % 2 * 32 + q * 4, 4))

    def table(k, grp, u, j):
        ph = ownphase if grp == 0 else zphase
        first = k % 2 * R
        fr = freqs[pl.ds(k, 1), mine] * (0.5 / jnp.pi)
        low1 = lax.broadcasted_iota(jnp.int32, (1, 2 * R), 1) < R
        frs = jnp.where(low1, fr, turn(fr)) if u == 0 else jnp.where(low1, turn(fr), fr)

        def one(q):
            o = j * Q + q
            if k % 2 == 0:
                picked = jnp.where(lane == o + first, ph[k // 2], 0.0)
            else:
                picked = jnp.where(lane == sub + first, ph[k // 2, pl.ds(o, 1)], 0.0)
            angle = jnp.sum(picked, axis=1, keepdims=True)
            t = angle * frs + quarter
            t = t - jnp.round(t)
            t2 = t * t
            p = SINE[5]
            for c in SINE[4::-1]:
                p = p * t2 + c
            tab[tab_at(k, grp, j, q)] = (p * t).astype(BF16).reshape(4, 16, 2 * R)

        for q in range(Q):
            one(q)

    def rotate(k, grp, j, q, p_, q_):
        t = tab[tab_at(k, grp, j, q)].reshape(R, 2 * R).astype(F32)
        r = turn(t)
        sine = jnp.where(low, t, r)
        cosine = jnp.where(low, r, t)
        return jnp.concatenate(
            [(cosine * p_ - sine * q_).astype(BF16), (sine * p_ + cosine * q_).astype(BF16)],
            axis=1)

    def mix(k, rows):
        return jnp.dot(jnp.concatenate(rows, axis=0), mixes[k], preferred_element_type=F32)

    def apart(k, grp, j, own, far, put):
        m = mats[k, pl.ds(0, 2 * R)]

        def pair(q):
            v = [jnp.concatenate([own[q + d], far[q + d]], axis=0) for d in range(2)]
            pq = jnp.dot(m, jnp.concatenate(v, axis=1), preferred_element_type=F32)
            rows = [
                rotate(k, grp, j, q + d, pq[:R, d * 2 * R:(d + 1) * 2 * R],
                       pq[R:, d * 2 * R:(d + 1) * 2 * R])
                for d in range(2)]
            v = mix(k, rows)
            for d in range(2):
                put(q + d, v[d * R:(d + 1) * R])

        for q in range(0, Q, 2):
            pair(q)

    def row_of(o):
        return pl.ds(pl.multiple_of(o * R, R), R)

    def put_f(grp, j):
        def put(q, v):
            f[grp, row_of(j * Q + q)] = v
        return put

    def level0(grp, u, j):
        i = u * N + j
        if grp == 0:
            @pl.when(j % 2 == 0)
            def _():
                y_own(i // 2).wait()
        else:
            y_copy(grp, i).wait()
        apart(0, grp, j, a.at[grp, i], y.at[grp, i], put_f(grp, j))

    def level1(u, j):
        m = mats[1]

        def pair(n):
            q = 2 * n
            v = []
            for d in range(2):
                o = j * Q + q + d
                v.append(jnp.concatenate(
                    [f[grp, pl.ds(o, R, stride=R)].astype(BF16) for grp in range(2)], axis=0))
            pq = jnp.dot(m, jnp.concatenate(v, axis=1), preferred_element_type=F32)
            for grp in range(2):
                rows = [
                    rotate(1, grp, j, q + d,
                           pq[grp * 2 * R:grp * 2 * R + R, d * 2 * R:(d + 1) * 2 * R],
                           pq[grp * 2 * R + R:(grp + 1) * 2 * R, d * 2 * R:(d + 1) * 2 * R])
                    for d in range(2)]
                w = mix(1, rows)
                for d in range(2):
                    g[grp, row_of(j * Q + q + d)] = w[d * R:(d + 1) * R]

        for n in range(Q // 2):
            pair(n)

    def core_send(u, j):
        for grp in range(2):
            for q in range(Q):
                y[grp, u * N + j, q] = g[grp, pl.ds(j * Q + q, R, stride=R)].astype(BF16)
        c_copy(u, j).start()

    def level2(u, j):
        c_copy(u, j).wait()
        for grp in range(2):
            apart(2, grp, j, y.at[grp, u * N + j], b2r.at[grp, u * N + j], put_f(grp, j))

    def x_pack(grp, u, j):
        for q in range(Q):
            a[grp, u * N + j, q] = f[grp, pl.ds(j * Q + q, R, stride=R)].astype(BF16)

    def x_send(u, j):
        x_pack(1, u, j)
        x_copy(1, u, j).start()
        x_pack(0, u, j)

    def level3(grp, u, j):
        i = u * N + j
        dst = a.at[0, i] if grp == 0 else s.at[i]

        def put(q, v):
            dst[q] = v.astype(BF16)

        x_copy(grp, u, j).wait()
        apart(3, grp, j, a.at[grp, i], b3r.at[grp, i], put)

    def merge(first, second, side, j, lanes):
        for q in range(Q):
            p0, p1 = first[q].astype(F32), second[q].astype(F32)
            out[0, j * Q + q, :, lanes] = jnp.where(low, p0, turn(p1)).astype(BF16)
            out[1, j * Q + q, :, lanes] = jnp.where(low, turn(p0), p1).astype(BF16)

    def z_arrive(i):
        z_fwd(i).wait()
        y_copy(1, i).start()

    def early(j):
        for k in range(4):
            table(k, 0, 0, j)
        level0(0, 0, j)

    loop(N, early)

    @pl.when(late == 1)
    def _():
        pl.semaphore_wait(gate, 1)
        loop(2 * N, lambda i: z_fwd(i).start())

    phase_copy().wait()

    def come(j):
        z_arrive(j)

        @pl.when((late == 0) & (j == 0))
        def _():
            pl.semaphore_signal(gate, inc=1, device_id=other, device_id_type=MESH)

        for k in range(4):
            table(k, 1, 0, j)

        @pl.when(j > 0)
        def _():
            level0(1, 0, j - 1)

    loop(N, come)
    loop(N // 2, lambda n: y_own(N // 2 + n).start())
    level0(1, 0, N - 1)

    loop(N, lambda j: level1(0, j))
    loop(4, lambda j: z_arrive(N + j))
    loop(N, lambda j: core_send(0, j))
    loop(N, lambda j: level2(0, j))
    loop(3, lambda j: z_arrive(N + 4 + j))
    loop(N, lambda j: x_send(0, j))
    z_arrive(2 * N - 1)

    def back0(j):
        level3(1, 0, j)
        z_back(j).start()
        x_copy(0, 0, j).start()
        for k in range(3):
            table(k, 0, 1, j)
            table(k, 1, 1, j)
        level0(0, 1, j)

    loop(N, back0)
    loop(N, lambda j: level0(1, 1, j))
    loop(N, lambda j: level1(1, j))
    loop(N, lambda j: core_send(1, j))
    loop(N, lambda j: level2(1, j))
    loop(N, lambda j: x_send(1, j))

    def end0(j):
        level3(0, 0, j)
        table(3, 0, 1, j)
        table(3, 1, 1, j)

    loop(N, end0)

    def back1(j):
        level3(1, 1, j)
        z_back(N + j).start()
        x_copy(0, 1, j).start()

    loop(N, back1)

    def own1(j):
        level3(0, 1, j)
        merge(a.at[0, j], a.at[0, N + j], 0, j, mine)

    loop(N, own1)

    def last(j):
        z_back(j).wait()
        z_back(N + j).wait()
        merge(zb.at[j], zb.at[N + j], 1, j, theirs)

    loop(N, last)


def local(field, phases, frequencies, self_mats, cross_mats, plane_mats):
    vm = pl.BlockSpec(memory_space=pltpu.VMEM)
    anywhere = pl.BlockSpec(memory_space=pl.ANY)
    chunk = (Q, R, 2 * R)
    unit2 = (2 * N,) + chunk
    dma = pltpu.SemaphoreType.DMA
    return pl.pallas_call(
        kernel,
        out_shape=pltpu.VMEM(field.shape, field.dtype),
        in_specs=[anywhere] * 6,
        out_specs=vm,
        scratch_shapes=[
            pltpu.VMEM(phases.shape, F32),
            pltpu.VMEM(frequencies.shape, F32),
            pltpu.VMEM(self_mats.shape, BF16),
            pltpu.VMEM(cross_mats.shape, BF16),
            pltpu.VMEM(plane_mats.shape, BF16),
            pltpu.VMEM((2, R, 2 * R), F32),
            pltpu.VMEM((2,) + unit2, BF16),
            pltpu.VMEM(unit2, BF16),
            pltpu.VMEM((2,) + unit2, BF16),
            pltpu.VMEM((2, R * R, 2 * R), F32),
            pltpu.VMEM((2, R * R, 2 * R), F32),
            pltpu.VMEM((2,) + unit2, BF16),
            pltpu.VMEM((2,) + unit2, BF16),
            pltpu.VMEM(unit2, BF16),
            pltpu.VMEM((16, 2, R, 16, 2 * R), BF16),
            pltpu.VMEM((2, R, 2 * R), F32),
            pltpu.VMEM((4, 4 * R, 2 * R), BF16),
            pltpu.VMEM((4, 4 * R, 2 * R), BF16),
            dma((8,)), dma, dma, dma((2 * N,)), dma((2 * N,)),
            dma((3 * N,)), dma((3 * N,)), dma((2 * N,)), dma((2 * N,)),
            dma((4 * N,)), dma((4 * N,)), dma((2 * N,)), dma((2 * N,)),
            dma((5,)), pltpu.SemaphoreType.REGULAR,
        ],
        compiler_params=pltpu.CompilerParams(
            collective_id=0, has_side_effects=True, vmem_limit_bytes=43 * 2**20),
        cost_estimate=pl.CostEstimate(
            flops=12 * 2**30, bytes_accessed=2**23, transcendentals=2**23),
    )(field, phases, frequencies, self_mats, cross_mats, plane_mats)


def solution(mesh):
    return jax.shard_map(
        local,
        mesh=mesh,
        in_specs=(P(None, "row", "col", None), P(None, "row", "col"), P(), P(), P(), P()),
        out_specs=P(None, "row", "col", None),
        check_vma=False,
    )
```

```python
import functools

import jax
import jax.numpy as jnp
from jax import lax
from jax.experimental import pallas as pl
from jax.experimental.pallas import tpu as pltpu
from jax.sharding import PartitionSpec as P

MESH = pl.DeviceIdType.MESH
F32 = jnp.float32
BF16 = jnp.bfloat16
R = 64
N = 8
Q = R // N
SINE = (
    6.283182621002197,
    -41.34142303466797,
    81.59618377685547,
    -76.5801010131836,
    41.20539093017578,
    -12.27125358581543,
)


def kernel(
    x, phases_in, freqs_in, selfs_in, crosses_in, planes_in, out,
    phases, freqs, selfs, crosses, planes, ownphase, a, s, y, f, g, b2r, b3r, zb, tab, zphase, mats, mixes,
    in_sem, ph_s, ph_r, zf_s, zf_r, y_s, y_r, c_s, c_r, x_s, x_r, zb_s, zb_r, mat_sem, gate,
):
    gr, gc = lax.axis_index("row"), lax.axis_index("col")
    nr, nc = lax.axis_size("row"), lax.axis_size("col")
    half = (gr // (nr // 2), gc // (nc // 2), gr % 2, gc % 2)
    to_y = (gr + nr // 2 - nr * half[0], gc)
    to_z = (gr, gc + nc // 2 - nc * half[1])
    to_c = (gr + 1 - 2 * half[2], gc)
    to_x = (gr, gc + 1 - 2 * half[3])
    other = (gr, (gc + nc // 4) % nc)
    late = (gc // (nc // 4)) % 2
    other_back = (gr, (gc + nc - nc // 4) % nc)

    def lanes_of(which):
        return pl.ds(pl.multiple_of(which * 2 * R, 2 * R), 2 * R)

    mine, theirs = lanes_of(half[1]), lanes_of(1 - half[1])

    def load_copy(n, side, lanes):
        return pltpu.make_async_copy(
            x.at[:, :, pl.ds(pl.multiple_of(n * 16, 16), 16), lanes],
            tab.at[side * 4 + n], in_sem.at[side * 4 + n])

    def remote(src, dst, ssem, rsem, to):
        return pltpu.make_async_remote_copy(
            src_ref=src, dst_ref=dst, send_sem=ssem, recv_sem=rsem,
            device_id=to, device_id_type=MESH)

    def phase_copy():
        return remote(ownphase, zphase, ph_s, ph_r, to_z)

    def small_copy(n):
        src = (phases_in, freqs_in, selfs_in, crosses_in, planes_in)[n]
        dst = (phases, freqs, selfs, crosses, planes)[n]
        return pltpu.make_async_copy(src, dst, mat_sem.at[n])

    def z_fwd(i):
        return remote(s.at[i], a.at[1, i], zf_s.at[i], zf_r.at[i], to_z)

    def y_copy(grp, i):
        return remote(a.at[grp, i], y.at[grp, i], y_s.at[i], y_r.at[i], to_y)

    def y_own(n):
        part = (0, pl.ds(2 * n, 2))
        return remote(a.at[part], y.at[part], y_s.at[2 * N + n], y_r.at[2 * N + n], to_y)

    def c_copy(u, j):
        n = u * N + j
        return remote(y.at[:, n], b2r.at[:, n], c_s.at[n], c_r.at[n], to_c)

    def x_copy(grp, u, j):
        n = grp * 2 * N + u * N + j
        return remote(a.at[grp, u * N + j], b3r.at[grp, u * N + j], x_s.at[n], x_r.at[n], to_x)

    def z_back(i):
        return remote(s.at[i], zb.at[i], zb_s.at[i], zb_r.at[i], to_z)

    def loop(n, body):
        lax.fori_loop(0, n, lambda i, c: (body(i), c)[1], 0)

    small_copy(0).start()
    for n in range(4):
        load_copy(n, 0, theirs).start()
    for n in range(4):
        load_copy(n, 1, mine).start()
    for n in range(1, 5):
        small_copy(n).start()

    barrier = pltpu.get_barrier_semaphore()
    for to in (to_y, to_z, to_c, to_x, other, other_back):
        pl.semaphore_signal(barrier, inc=1, device_id=to, device_id_type=MESH)

    lane = lax.broadcasted_iota(jnp.int32, (R, 2 * R), 1)
    low = lane < R

    def turn(v):
        return pltpu.roll(v, R, 1)

    def pack(n, side, put):
        f[0, pl.ds(0, R * 16)] = tab[side * 4 + n, 0].reshape(R * 16, 2 * R).astype(F32)
        f[1, pl.ds(0, R * 16)] = tab[side * 4 + n, 1].reshape(R * 16, 2 * R).astype(F32)
        for k in range(16):
            re = f[0, pl.ds(k, R, stride=16)]
            im = f[1, pl.ds(k, R, stride=16)]
            put(n * 2 + k // Q, k % Q,
                jnp.where(low, re, turn(im)).astype(BF16),
                jnp.where(low, turn(re), im).astype(BF16))

    def put_s(j, k, first, second):
        s[j, k] = first
        s[N + j, k] = second

    def put_a(j, k, first, second):
        a[0, j, k] = first
        a[0, N + j, k] = second

    def pack_theirs(n):
        load_copy(n, 0, theirs).wait()
        pack(n, 0, put_s)

    def pack_mine(n):
        load_copy(n, 1, mine).wait()
        pack(n, 1, put_a)
        y_own(n).start()

    small_copy(0).wait()
    for k in range(2):
        ownphase[k] = jnp.concatenate([phases[2 * k], phases[2 * k + 1]], axis=1)
    pl.semaphore_wait(barrier, 6)
    phase_copy().start()
    pack_theirs(0)

    @pl.when(late == 0)
    def _():
        z_fwd(0).start()
        z_fwd(1).start()

    def pack_next(n):
        pack_theirs(n + 1)

        @pl.when(late == 0)
        def _():
            z_fwd(2 * n + 2).start()
            z_fwd(2 * n + 3).start()

    loop(3, pack_next)

    @pl.when(late == 0)
    def _():
        loop(N, lambda j: z_fwd(N + j).start())

    loop(4, pack_mine)

    for n in range(1, 5):
        small_copy(n).wait()
    for k in range(4):
        h = half[k]
        own = selfs[k, h]
        far = crosses[k, h]
        if k == 1:
            own2 = selfs[k, 1 - h]
            far2 = crosses[k, 1 - h]
            rows = [(own, far), (far2, own2)]
        else:
            rows = [(own, far)]
        blocks = []
        for left, right in rows:
            for part in range(2):
                blocks.append(jnp.concatenate(
                    [left[part].astype(F32), right[part].astype(F32)], axis=1))
        m = jnp.concatenate(blocks, axis=0)
        mats[k, pl.ds(0, m.shape[0])] = m.astype(BF16)
        re, im = planes[k, 0].astype(F32), planes[k, 1].astype(F32)
        wide = jnp.concatenate([
            jnp.concatenate([re, -im, -im, -re], axis=1),
            jnp.concatenate([im, re, re, -im], axis=1)], axis=0)
        mixes[k] = wide.T.astype(BF16)

    sub = lax.broadcasted_iota(jnp.int32, (R, 2 * R), 0)
    quarter = jnp.where(low, 0.0, 0.25)

    def tab_at(k, grp, j, q):
        return ((k * 2 + grp) * 2 + j // 4, j // 2 % 2, pl.ds(j % 2 * 32 + q * 4, 4))

    def table(k, grp, u, j):
        ph = ownphase if grp == 0 else zphase
        first = k % 2 * R
        fr = freqs[pl.ds(k, 1), mine] * (0.5 / jnp.pi)
        low1 = lax.broadcasted_iota(jnp.int32, (1, 2 * R), 1) < R
        frs = jnp.where(low1, fr, turn(fr)) if u == 0 else jnp.where(low1, turn(fr), fr)

        def one(q):
            o = j * Q + q
            if k % 2 == 0:
                picked = jnp.where(lane == o + first, ph[k // 2], 0.0)
            else:
                picked = jnp.where(lane == sub + first, ph[k // 2, pl.ds(o, 1)], 0.0)
            angle = jnp.sum(picked, axis=1, keepdims=True)
            t = angle * frs + quarter
            t = t - jnp.round(t)
            t2 = t * t
            p = SINE[5]
            for c in SINE[4::-1]:
                p = p * t2 + c
            tab[tab_at(k, grp, j, q)] = (p * t).astype(BF16).reshape(4, 16, 2 * R)

        for q in range(Q):
            one(q)

    def rotate(k, grp, j, q, p_, q_):
        t = tab[tab_at(k, grp, j, q)].reshape(R, 2 * R).astype(F32)
        r = turn(t)
        sine = jnp.where(low, t, r)
        cosine = jnp.where(low, r, t)
        return jnp.concatenate(
            [(cosine * p_ - sine * q_).astype(BF16), (sine * p_ + cosine * q_).astype(BF16)],
            axis=1)

    def mix(k, rows):
        return jnp.dot(jnp.concatenate(rows, axis=0), mixes[k], preferred_element_type=F32)

    def apart(k, grp, j, own, far, put):
        m = mats[k, pl.ds(0, 2 * R)]

        def pair(q):
            v = [jnp.concatenate([own[q + d], far[q + d]], axis=0) for d in range(2)]
            pq = jnp.dot(m, jnp.concatenate(v, axis=1), preferred_element_type=F32)
            rows = [
                rotate(k, grp, j, q + d, pq[:R, d * 2 * R:(d + 1) * 2 * R],
                       pq[R:, d * 2 * R:(d + 1) * 2 * R])
                for d in range(2)]
            v = mix(k, rows)
            for d in range(2):
                put(q + d, v[d * R:(d + 1) * R])

        for q in range(0, Q, 2):
            pair(q)

    def row_of(o):
        return pl.ds(pl.multiple_of(o * R, R), R)

    def put_f(grp, j):
        def put(q, v):
            f[grp, row_of(j * Q + q)] = v
        return put

    def level0(grp, u, j):
        i = u * N + j
        if grp == 0:
            @pl.when(j % 2 == 0)
            def _():
                y_own(i // 2).wait()
        else:
            y_copy(grp, i).wait()
        apart(0, grp, j, a.at[grp, i], y.at[grp, i], put_f(grp, j))

    def level1(u, j):
        m = mats[1]

        def pair(n):
            q = 2 * n
            v = []
            for d in range(2):
                o = j * Q + q + d
                v.append(jnp.concatenate(
                    [f[grp, pl.ds(o, R, stride=R)].astype(BF16) for grp in range(2)], axis=0))
            pq = jnp.dot(m, jnp.concatenate(v, axis=1), preferred_element_type=F32)
            for grp in range(2):
                rows = [
                    rotate(1, grp, j, q + d,
                           pq[grp * 2 * R:grp * 2 * R + R, d * 2 * R:(d + 1) * 2 * R],
                           pq[grp * 2 * R + R:(grp + 1) * 2 * R, d * 2 * R:(d + 1) * 2 * R])
                    for d in range(2)]
                w = mix(1, rows)
                for d in range(2):
                    g[grp, row_of(j * Q + q + d)] = w[d * R:(d + 1) * R]

        for n in range(Q // 2):
            pair(n)

    def core_send(u, j):
        for grp in range(2):
            for q in range(Q):
                y[grp, u * N + j, q] = g[grp, pl.ds(j * Q + q, R, stride=R)].astype(BF16)
        c_copy(u, j).start()

    def level2(u, j):
        c_copy(u, j).wait()
        for grp in range(2):
            apart(2, grp, j, y.at[grp, u * N + j], b2r.at[grp, u * N + j], put_f(grp, j))

    def x_pack(grp, u, j):
        for q in range(Q):
            a[grp, u * N + j, q] = f[grp, pl.ds(j * Q + q, R, stride=R)].astype(BF16)

    def x_send(u, j):
        x_pack(1, u, j)
        x_copy(1, u, j).start()
        x_pack(0, u, j)

    def level3(grp, u, j):
        i = u * N + j
        dst = a.at[0, i] if grp == 0 else s.at[i]

        def put(q, v):
            dst[q] = v.astype(BF16)

        x_copy(grp, u, j).wait()
        apart(3, grp, j, a.at[grp, i], b3r.at[grp, i], put)

    def merge(first, second, side, j, lanes):
        for q in range(Q):
            p0, p1 = first[q].astype(F32), second[q].astype(F32)
            out[0, j * Q + q, :, lanes] = jnp.where(low, p0, turn(p1)).astype(BF16)
            out[1, j * Q + q, :, lanes] = jnp.where(low, turn(p0), p1).astype(BF16)

    def z_arrive(i):
        z_fwd(i).wait()
        y_copy(1, i).start()

    def early(j):
        for k in range(4):
            table(k, 0, 0, j)
        level0(0, 0, j)

    loop(N, early)

    @pl.when(late == 1)
    def _():
        pl.semaphore_wait(gate, 1)
        loop(2 * N, lambda i: z_fwd(i).start())

    phase_copy().wait()

    def come(j):
        z_arrive(j)

        @pl.when((late == 0) & (j == 0))
        def _():
            pl.semaphore_signal(gate, inc=1, device_id=other, device_id_type=MESH)

        for k in range(4):
            table(k, 1, 0, j)

        @pl.when(j > 0)
        def _():
            level0(1, 0, j - 1)

    loop(N, come)
    loop(N // 2, lambda n: y_own(N // 2 + n).start())
    level0(1, 0, N - 1)

    loop(N, lambda j: level1(0, j))
    loop(4, lambda j: z_arrive(N + j))
    loop(N, lambda j: core_send(0, j))
    loop(N, lambda j: level2(0, j))
    loop(3, lambda j: z_arrive(N + 4 + j))
    loop(N, lambda j: x_send(0, j))
    z_arrive(2 * N - 1)

    def back0(j):
        level3(1, 0, j)
        z_back(j).start()
        x_copy(0, 0, j).start()
        for k in range(3):
            table(k, 0, 1, j)
            table(k, 1, 1, j)
        level0(0, 1, j)

    loop(N, back0)
    loop(N, lambda j: level0(1, 1, j))
    loop(N, lambda j: level1(1, j))
    loop(N, lambda j: core_send(1, j))
    loop(N, lambda j: level2(1, j))
    loop(N, lambda j: x_send(1, j))

    def end0(j):
        level3(0, 0, j)
        table(3, 0, 1, j)
        table(3, 1, 1, j)

    loop(N, end0)

    def back1(j):
        level3(1, 1, j)
        z_back(N + j).start()
        x_copy(0, 1, j).start()

    loop(N, back1)

    def own1(j):
        level3(0, 1, j)
        merge(a.at[0, j], a.at[0, N + j], 0, j, mine)

    loop(N, own1)

    def last(j):
        z_back(j).wait()
        z_back(N + j).wait()
        merge(zb.at[j], zb.at[N + j], 1, j, theirs)

    loop(N, last)


def local(field, phases, frequencies, self_mats, cross_mats, plane_mats):
    vm = pl.BlockSpec(memory_space=pltpu.VMEM)
    anywhere = pl.BlockSpec(memory_space=pl.ANY)
    chunk = (Q, R, 2 * R)
    unit2 = (2 * N,) + chunk
    dma = pltpu.SemaphoreType.DMA
    return pl.pallas_call(
        kernel,
        out_shape=pltpu.VMEM(field.shape, field.dtype),
        in_specs=[anywhere] * 6,
        out_specs=vm,
        scratch_shapes=[
            pltpu.VMEM(phases.shape, F32),
            pltpu.VMEM(frequencies.shape, F32),
            pltpu.VMEM(self_mats.shape, BF16),
            pltpu.VMEM(cross_mats.shape, BF16),
            pltpu.VMEM(plane_mats.shape, BF16),
            pltpu.VMEM((2, R, 2 * R), F32),
            pltpu.VMEM((2,) + unit2, BF16),
            pltpu.VMEM(unit2, BF16),
            pltpu.VMEM((2,) + unit2, BF16),
            pltpu.VMEM((2, R * R, 2 * R), F32),
            pltpu.VMEM((2, R * R, 2 * R), F32),
            pltpu.VMEM((2,) + unit2, BF16),
            pltpu.VMEM((2,) + unit2, BF16),
            pltpu.VMEM(unit2, BF16),
            pltpu.VMEM((16, 2, R, 16, 2 * R), BF16),
            pltpu.VMEM((2, R, 2 * R), F32),
            pltpu.VMEM((4, 4 * R, 2 * R), BF16),
            pltpu.VMEM((4, 4 * R, 2 * R), BF16),
            dma((8,)), dma, dma, dma((2 * N,)), dma((2 * N,)),
            dma((3 * N,)), dma((3 * N,)), dma((2 * N,)), dma((2 * N,)),
            dma((4 * N,)), dma((4 * N,)), dma((2 * N,)), dma((2 * N,)),
            dma((5,)), pltpu.SemaphoreType.REGULAR,
        ],
        compiler_params=pltpu.CompilerParams(
            collective_id=0, has_side_effects=True, vmem_limit_bytes=58 * 2**20),
        cost_estimate=pl.CostEstimate(
            flops=12 * 2**30, bytes_accessed=2**23, transcendentals=2**23),
    )(field, phases, frequencies, self_mats, cross_mats, plane_mats)


def solution(mesh):
    return jax.shard_map(
        local,
        mesh=mesh,
        in_specs=(P(None, "row", "col", None), P(None, "row", "col"), P(), P(), P(), P()),
        out_specs=P(None, "row", "col", None),
        check_vma=False,
    )
```
